32 devices in a mesh: tile: 8 (over z, x), lev: 4 (over y, core).
Axes of the slice: x: 2, y: 2, z: 4, core: 2. Of those that a mesh axis runs over, the one named last changes fastest.
Arguments:
- ocean_state: bfloat16 [4, 128, 256, 128], P('lev', 'tile'), may hold values from -6 to 6
- tile_owner: int32 [8, 16], replicated, may hold values from -1 to 63, as said below
- kernel: bfloat16 [7, 7, 128], replicated, may hold values from -0.875 to 0.875
- bias_dw: float32 [128], replicated, may hold values from -3 to 3
- ln_gain: float32 [128], replicated, may hold values from 0.5 to 2
- ln_bias: float32 [128], replicated, may hold values from -3 to 3
- w_in: bfloat16 [128, 512], replicated, may hold values from -0.5 to 0.5
- b_in: float32 [512], replicated, may hold values from -3 to 3
- w_out: bfloat16 [512, 128], replicated, may hold values from -0.25 to 0.25
- b_out: float32 [128], replicated, may hold values from -3 to 3
- layer_scale: float32 [128], replicated, may hold values from 0.3 to 1.5
- w_vert: bfloat16 [5, 128, 128], replicated, may hold values from -0.25 to 0.25
Outputs:
- updated: bfloat16 [64, 4, 256, 128], P('tile', None, 'lev')
The draws below stay inside these ranges and needn't reach their ends.
Inputs may be any that keep to these rules, and one draw needn't show every extreme that they name: `tile_owner`: every value from 0 to 63 appears exactly once; -1 marks a land tile. Value g names owner g // 8, so every owner receives exactly 8 tiles. No latitude row sends more than 2 tiles to one owner, and in every draw some row sends exactly 2 to some owner.
All inputs are finite; a program needn't handle non-finite values.
Results may differ from the reference program's by a relative error of at most 0.006.
Values may be sent and summed in bfloat16 or wider, within the bound.
A program may use at most 64 MiB of HBM per device.

```python
import math
import jax
import jax.numpy as jnp
from jax import lax

C = 128
HID = 512
TS = 16
KS = 7
VK = 5
CAP = 2
LEVELS = 4
NLAT = 8
NLON = 16
OWN = 8
WET = 64


def draw_tile_owner(key, part):
    band_count = NLAT
    keys = jax.random.split(key, 4)
    quarter = max(band_count // 4, 1)
    base_tilt = jnp.concatenate([jnp.ones((quarter,), jnp.int32), -jnp.ones((quarter,), jnp.int32), jnp.zeros((band_count - 2 * quarter,), jnp.int32)])
    tilt = jax.random.permutation(keys[0], base_tilt)
    lifted = jax.random.randint(keys[1], (band_count,), 0, 2).astype(jnp.int32)
    chosen = jax.random.randint(keys[2], (), 0, band_count)
    lifted = jnp.where(jnp.arange(band_count) == chosen, 1, lifted).astype(jnp.int32)
    pair_count = 1 + tilt[:, None] * lifted[None, :]
    first_slot = jnp.cumsum(pair_count, axis=0) - pair_count
    entry_dest = jnp.repeat(jnp.arange(band_count, dtype=jnp.int32), CAP)
    entry_rank = jnp.tile(jnp.arange(CAP, dtype=jnp.int32), band_count)
    valid = entry_rank[None, :] < pair_count[:, entry_dest]
    value = entry_dest[None, :] * OWN + first_slot[:, entry_dest] + entry_rank[None, :]
    order_key = jnp.where(valid, 0, 1).astype(jnp.int32)
    arranged_order = jnp.argsort(order_key, axis=1, stable=True)
    arranged = jnp.take_along_axis(jnp.where(valid, value, -1), arranged_order, axis=1)
    row_keys = jax.random.split(keys[3], band_count)
    places = jax.vmap(lambda row_key: jax.random.permutation(row_key, NLON))(row_keys)
    inverse = jnp.argsort(places, axis=1)
    return jnp.take_along_axis(arranged, inverse, axis=1).astype(jnp.int32)


def steps_of(stream_key, extent, cuts, least, high):
    level, own = 1.0, jax.random.fold_in(stream_key, 6)
    for position, parts in cuts:
        steps = jnp.exp(jax.random.uniform(jax.random.fold_in(own, position), (parts,), jnp.float32, least / len(cuts), high / len(cuts)))
        level = level * jnp.repeat(steps, extent[position] // parts).reshape([-1 if axis == position else 1 for axis in range(len(extent))])
    return level


def scatter_about(key, dims, deviation, bound, shards=(), held_as=jnp.bfloat16):
    gain = steps_of(key, dims, shards, -0.22, 0.18) if shards else 1.0
    entries = jax.random.normal(key, dims, jnp.float32) * deviation * gain
    return jnp.minimum(jnp.maximum(entries, -bound), bound).astype(held_as)


def setup_inputs(seed: int = 0) -> dict:
    key_list = jax.random.split(jax.random.key(seed), 13)
    ocean_state = scatter_about(key_list[0], (LEVELS, NLAT * TS, NLON * TS, C), 1.0, 6.0, ((0, 4), (1, 8)))
    tile_owner = draw_tile_owner(jax.random.fold_in(key_list[12], 71), 0)
    kernel = scatter_about(key_list[2], (KS, KS, C), (KS * KS) ** -0.5, 0.875)
    bias_dw = scatter_about(key_list[3], (C,), 0.5, 3.0, (), jnp.float32)
    ln_gain = jnp.clip(jnp.exp(jax.random.uniform(key_list[4], (C,), jnp.float32, math.log(0.5), math.log(2.0))), 0.5, 2.0)
    ln_bias = scatter_about(key_list[5], (C,), 0.5, 3.0, (), jnp.float32)
    w_in = scatter_about(key_list[6], (C, HID), C ** -0.5, 0.5)
    b_in = scatter_about(key_list[7], (HID,), 0.5, 3.0, (), jnp.float32)
    w_out = scatter_about(key_list[8], (HID, C), HID ** -0.5, 0.25)
    b_out = scatter_about(key_list[9], (C,), 0.5, 3.0, (), jnp.float32)
    layer_scale = jnp.clip(jnp.exp(jax.random.uniform(key_list[10], (C,), jnp.float32, math.log(0.3), math.log(1.5))), 0.3, 1.5)
    w_vert = scatter_about(key_list[11], (VK, C, C), (VK * C) ** -0.5, 0.25)
    return dict(ocean_state=ocean_state, tile_owner=tile_owner, kernel=kernel, bias_dw=bias_dw, ln_gain=ln_gain, ln_bias=ln_bias, w_in=w_in, b_in=b_in, w_out=w_out, b_out=b_out, layer_scale=layer_scale, w_vert=w_vert)


def depthwise(padded, kernel, bias_dw, rows, cols):
    total = jnp.zeros(padded.shape[:-3] + (rows, cols, padded.shape[-1]), jnp.float32) + bias_dw.astype(jnp.float32)
    for i in range(7):
        for j in range(7):
            total = total + padded[..., i:i + rows, j:j + cols, :].astype(jnp.float32) * kernel[i, j].astype(jnp.float32)
    return total.astype(jnp.bfloat16)

def feed_forward(conv_rows, input_rows, ln_gain, ln_bias, w_in, b_in, w_out, b_out, layer_scale):
    values = conv_rows.astype(jnp.float32)
    centre = lax.optimization_barrier(jnp.mean(values, axis=-1, keepdims=True))
    spread = lax.optimization_barrier(jnp.mean((values - centre) ** 2, axis=-1, keepdims=True))
    normed = ((values - centre) / jnp.sqrt(spread + 1e-06) * ln_gain + ln_bias).astype(jnp.bfloat16)
    hidden = jax.nn.gelu(jnp.dot(normed, w_in, preferred_element_type=jnp.float32) + b_in, approximate=False).astype(jnp.bfloat16)
    branch = jnp.dot(hidden, w_out, preferred_element_type=jnp.float32) + b_out
    return (input_rows.astype(jnp.float32) + layer_scale * branch).astype(jnp.bfloat16)

def vertical(block_mid, w_vert):
    level_count = block_mid.shape[-3]
    widths = [(0, 0)] * (block_mid.ndim - 3) + [(2, 2), (0, 0), (0, 0)]
    level_pad = jnp.pad(block_mid, widths)
    channels = block_mid.shape[-1]
    total = block_mid.astype(jnp.float32)
    for k in range(5):
        taken = level_pad[..., k:k + level_count, :, :].reshape(-1, channels)
        total = total + jnp.dot(taken, w_vert[k], preferred_element_type=jnp.float32).reshape(block_mid.shape)
    return total.astype(jnp.bfloat16)

def reference(ocean_state, tile_owner, kernel, bias_dw, ln_gain, ln_bias, w_in, b_in, w_out, b_out, layer_scale, w_vert):
    wet_cells = jnp.repeat(jnp.repeat(tile_owner >= 0, TS, axis=0), TS, axis=1)
    masked = jnp.where(wet_cells[None, :, :, None], ocean_state, jnp.zeros((), jnp.bfloat16))

    def one_level(level):
        padded = jnp.pad(level, ((3, 3), (0, 0), (0, 0)))
        padded = jnp.concatenate([padded[:, -3:], padded, padded[:, :3]], axis=1)
        return depthwise(padded, kernel, bias_dw, NLAT * TS, NLON * TS)
    conv_out = lax.map(one_level, masked)

    def to_tiles(field_in):
        shaped = field_in.reshape(LEVELS, NLAT, TS, NLON, TS, C).transpose(1, 3, 0, 2, 4, 5)
        return shaped.reshape(NLAT * NLON, LEVELS, TS * TS, C)
    owner_flat = tile_owner.reshape(-1)
    slot_index = jnp.where(owner_flat >= 0, owner_flat, WET).astype(jnp.int32)
    order_index = jnp.zeros((WET,), jnp.int32).at[slot_index].set(jnp.arange(NLAT * NLON, dtype=jnp.int32), mode='drop')
    tile_conv = to_tiles(conv_out)[order_index]
    tile_input = to_tiles(masked)[order_index]

    def apply_tile(blocks):
        conv_rows = blocks[0].reshape(-1, C)
        input_rows = blocks[1].reshape(-1, C)
        block_mid = feed_forward(conv_rows, input_rows, ln_gain, ln_bias, w_in, b_in, w_out, b_out, layer_scale)
        return vertical(block_mid.reshape(LEVELS, TS * TS, C), w_vert)
    return lax.map(apply_tile, (tile_conv, tile_input))
```

```python
import jax
import jax.numpy as jnp
from jax import lax
from jax.experimental import pallas as pl
from jax.experimental.pallas import tpu as pltpu
from jax.sharding import PartitionSpec as P

CAP = 2


def block_kernel(
    pick_ref,
    present_ref,
    field_ref,
    taps_ref,
    bias_ref,
    gain_ref,
    shift_ref,
    w_in_ref,
    b_in_ref,
    w_out_ref,
    b_out_ref,
    scale_ref,
    out_ref,
    window,
):
    slot = pl.program_id(0)
    level = pl.program_id(1)
    side = window.shape[0] - 6
    channels = window.shape[2]
    half = side // 2

    @pl.when(present_ref[slot] > 0)
    def _():
        start = pl.multiple_of(pick_ref[slot] * side, side)
        window[...] = field_ref[level, :, pl.ds(start, 2 * side), :].astype(jnp.float32)
        parts = []
        for top in (0, half):
            total = jnp.zeros((half, side, channels), jnp.float32) + bias_ref[...][None]
            for j in range(7):
                column = window[top : top + half + 6, j : j + side, :]
                for i in range(7):
                    tap = taps_ref[i * 7 + j : i * 7 + j + 1, :]
                    total = total + column[i : i + half] * tap[None]
            parts.append(total.reshape(half * side, channels))
        values = jnp.concatenate(parts, axis=0).astype(jnp.bfloat16).astype(jnp.float32)
        centre = jnp.mean(values, axis=-1, keepdims=True)
        offset = values - centre
        spread = jnp.mean(offset * offset, axis=-1, keepdims=True)
        normed = offset * lax.rsqrt(spread + 1e-06) * gain_ref[...] + shift_ref[...]
        wide = (
            jnp.dot(
                normed.astype(jnp.bfloat16), w_in_ref[...], preferred_element_type=jnp.float32
            )
            + b_in_ref[...]
        )
        size = jnp.abs(wide)
        t = 1.0 / (1.0 + 0.231641888 * size)
        poly = t * (
            0.127414796
            + t * (-0.142248368 + t * (0.7107068705 + t * (-0.7265760135 + t * 0.5307027145)))
        )
        tail = poly * jnp.exp(-0.5 * wide * wide)
        hidden = (jnp.maximum(wide, 0.0) - size * tail).astype(jnp.bfloat16)
        branch = (
            jnp.dot(hidden, w_out_ref[...], preferred_element_type=jnp.float32) + b_out_ref[...]
        )
        inner = window[3 : 3 + side, 3 : 3 + side, :].reshape(side * side, channels)
        mid = (inner + scale_ref[...] * branch).astype(jnp.bfloat16)
        out_ref[...] = mid.reshape(out_ref.shape)


def block_slots(padded, pick_index, present, taps, params, tile_count, lev_count):
    levels, rows, width, channels = padded.shape
    side = rows - 6
    share = side * side // lev_count
    slots = pick_index.shape[0]
    bias_dw, ln_gain, ln_bias, w_in, b_in, w_out, b_out, layer_scale = params

    def row(vector):
        return vector.reshape(1, -1)

    operands = (
        padded,
        taps.astype(jnp.float32).reshape(-1, channels),
        row(bias_dw),
        row(ln_gain),
        row(ln_bias),
        w_in,
        row(b_in),
        w_out,
        row(b_out),
        row(layer_scale),
    )

    def whole(operand):
        dims = operand.ndim
        return pl.BlockSpec(operand.shape, lambda s, l, *_: (0,) * dims)

    return pl.pallas_call(
        block_kernel,
        out_shape=jax.ShapeDtypeStruct(
            (tile_count, lev_count, CAP * levels, share, channels), jnp.bfloat16
        ),
        grid_spec=pltpu.PrefetchScalarGridSpec(
            num_scalar_prefetch=2,
            grid=(slots, levels),
            in_specs=[whole(operand) for operand in operands],
            out_specs=pl.BlockSpec(
                (1, lev_count, 1, share, channels),
                lambda s, l, *_: (s // CAP, 0, (s % CAP) * levels + l, 0, 0),
            ),
            scratch_shapes=[pltpu.VMEM((rows, 2 * side, channels), jnp.float32)],
        ),
        compiler_params=pltpu.CompilerParams(vmem_limit_bytes=40 * 1024 * 1024),
    )(pick_index.astype(jnp.int32), present.astype(jnp.int32), *operands)


def padded_rows(cells, axis, width):
    count = lax.axis_size(axis)
    ends = count - 1
    above = lax.ppermute(cells[:, -width:], axis, [(i, i + 1) for i in range(ends)])
    below = lax.ppermute(cells[:, :width], axis, [(i + 1, i) for i in range(ends)])
    return jnp.concatenate([above, cells, below], axis=1)


def vertical(block_mid, w_vert):
    level_count = block_mid.shape[-3]
    widths = [(0, 0)] * (block_mid.ndim - 3) + [(2, 2), (0, 0), (0, 0)]
    level_pad = jnp.pad(block_mid, widths)
    channels = block_mid.shape[-1]
    total = block_mid.astype(jnp.float32)
    for k in range(5):
        taken = level_pad[..., k : k + level_count, :, :].reshape(-1, channels)
        total = total + jnp.dot(taken, w_vert[k], preferred_element_type=jnp.float32).reshape(
            block_mid.shape
        )
    return total.astype(jnp.bfloat16)


def body(
    ocean_state,
    tile_owner,
    kernel,
    bias_dw,
    ln_gain,
    ln_bias,
    w_in,
    b_in,
    w_out,
    b_out,
    layer_scale,
    w_vert,
):
    tile_count = lax.axis_size("tile")
    band_index = lax.axis_index("tile")
    local_levels, tile_side, lon_cells, channels = ocean_state.shape
    lon_tiles = tile_owner.shape[1]
    per_owner = tile_owner.shape[0]
    tile_cells = tile_side * tile_side
    lev_count = lax.axis_size("lev")
    params = (bias_dw, ln_gain, ln_bias, w_in, b_in, w_out, b_out, layer_scale)
    dest_all = jnp.where(tile_owner >= 0, tile_owner // per_owner, -1)
    same_dest = (dest_all[:, :, None] == dest_all[:, None, :]) & (tile_owner[:, :, None] >= 0)
    positions = jnp.arange(lon_tiles, dtype=jnp.int32)
    earlier = positions[None, :] < positions[:, None]
    rank_all = jnp.sum((same_dest & earlier[None]).astype(jnp.int32), axis=2)
    my_owner = lax.dynamic_index_in_dim(tile_owner, band_index, 0, keepdims=False)
    my_dest = lax.dynamic_index_in_dim(dest_all, band_index, 0, keepdims=False)
    my_rank = lax.dynamic_index_in_dim(rank_all, band_index, 0, keepdims=False)
    wet_cols = jnp.repeat(my_owner >= 0, tile_side)
    masked = jnp.where(wet_cols[None, None, :, None], ocean_state, jnp.zeros((), ocean_state.dtype))
    padded = padded_rows(masked, "tile", 3)
    padded = jnp.concatenate(
        [padded[:, :, -3:], padded, padded[:, :, : tile_side - 3]], axis=2
    )

    slot_ids = jnp.arange(tile_count * CAP, dtype=jnp.int32)
    match_table = (my_dest[None, :] == (slot_ids // CAP)[:, None]) & (
        my_rank[None, :] == (slot_ids % CAP)[:, None]
    )
    pick_index = jnp.argmax(match_table.astype(jnp.int32), axis=1)
    present = jnp.any(match_table, axis=1)
    owner_flat = tile_owner.reshape(-1)
    target = band_index * per_owner + jnp.arange(per_owner, dtype=jnp.int32)
    hit_table = (owner_flat[None, :] == target[:, None]).astype(jnp.int32)
    src_flat = jnp.argmax(hit_table, axis=1)
    src_band = src_flat // lon_tiles
    src_rank = rank_all.reshape(-1)[src_flat]
    selected = block_slots(padded, pick_index, present, kernel, params, tile_count, lev_count)
    share = tile_cells // lev_count
    received = lax.all_to_all(
        selected.reshape(tile_count * lev_count, CAP * local_levels, share, channels),
        ("tile", "lev"),
        split_axis=0,
        concat_axis=0,
        tiled=True,
    ).reshape(tile_count, lev_count, CAP, local_levels, share, channels)
    block_mid = received.transpose(0, 2, 1, 3, 4, 5).reshape(
        tile_count * CAP, lev_count * local_levels, share, channels
    )[src_band * CAP + src_rank]
    return vertical(block_mid, w_vert)


def solution(mesh):
    return jax.shard_map(
        body,
        mesh=mesh,
        in_specs=(
            P("lev", "tile", None, None),
            P(),
            P(),
            P(),
            P(),
            P(),
            P(),
            P(),
            P(),
            P(),
            P(),
            P(),
        ),
        out_specs=P("tile", None, "lev", None),
        check_vma=False,
    )
```
